512 devices in a mesh: frame: 64 (over x, y, z_hi), head: 8 (over z_lo, core).
Axes of the slice: x: 4, y: 8, z: 8 (z_hi: 2, z_lo: 4; z = z_hi * 4 + z_lo), core: 2. Of those that a mesh axis runs over, the one named last changes fastest.
Arguments:
- queries: bfloat16 [49152, 5120], P('frame', 'head'), may hold values from -4.5 to 4.5
- keys: bfloat16 [49152, 5120], P('frame', 'head'), may hold values from -4.5 to 4.5
- values: bfloat16 [49152, 5120], P('frame', 'head'), may hold values from -6 to 6
- image_slots: bfloat16 [64, 2, 512, 5120], P('frame', None, None, 'head'), may hold values from -6 to 6
- owner: int32 [1], replicated, may hold values from 0 to 63
- pattern: int32 [192, 5], P('frame'), may hold values from -1 to 191, as said below
Outputs:
- attended: bfloat16 [49152, 5120], P('frame', 'head')
The draws below stay inside these ranges and needn't reach their ends.
Inputs may be any that keep to these rules, and one draw needn't show every extreme that they name: `pattern`: entry j of tile t's list is t + j - 2 or -1; entry 2 is always t, and entries that would leave the range 0 to 191 are -1.
All inputs are finite; a program needn't handle non-finite values.
Results may differ from the reference program's by a relative error of at most 0.0035.
Values may be sent and summed in bfloat16 or wider, within the bound.
No kernel may reach another device: no remote copies, remote signals or barrier semaphores. Data moves between devices by JAX's collectives and lax.ppermute only.
A program may use at most 128 MiB of HBM per device.

```python
import jax
import jax.numpy as jnp
from jax import lax

HEADS = 40
DH = 128
TILE = 256
REACH = 2
REF = 512
NB = 5
TILES = 192
TOKENS = 49152
N_FRAME = 64


def aligned_rows(key):
    first, second, third = jax.random.split(key, 3)
    picked = jax.random.randint(first, (TOKENS,), 0, 64) == 0
    signs = jnp.where(jax.random.bernoulli(second, 0.5, (HEADS * DH,)), 1.0, -1.0)
    strength = jax.random.uniform(third, (TOKENS,), jnp.float32, 3.2, 4.4)
    return (picked, signs, strength)


def draw_queries(key, part):
    picked, signs, strength = aligned_rows(key)
    key = jax.random.fold_in(key, 11)
    base = jnp.clip(jax.random.normal(key, (TOKENS, HEADS * DH), jnp.float32), -4.5, 4.5)
    out = jnp.where(picked[:, None], strength[:, None] * signs[None, :], base)
    return out.astype(jnp.bfloat16)


def draw_keys(key, part):
    key = jax.random.fold_in(key, 23)
    out = jnp.clip(jax.random.normal(key, (TOKENS, HEADS * DH), jnp.float32), -4.5, 4.5)
    return out.astype(jnp.bfloat16)


def draw_pattern(key, part):
    key = jax.random.fold_in(key, 37)
    tiles = jnp.arange(TILES, dtype=jnp.int32)[:, None]
    offsets = jnp.arange(NB, dtype=jnp.int32)[None, :] - REACH
    kept = jax.random.randint(key, (TILES, NB), 0, 4) > 0
    target = tiles + offsets
    inside = (target >= 0) & (target < TILES)
    keep = inside & (kept | (offsets == 0))
    return jnp.where(keep, target, -1).astype(jnp.int32)


def level_of(own_key, extent, shards, least, high):
    factor_of = 1.0
    for dim, blocks in shards:
        heights = jax.random.uniform(jax.random.fold_in(jax.random.fold_in(own_key, 6), dim), (blocks,), jnp.float32, least / len(shards), high / len(shards))
        factor_of = factor_of * jnp.repeat(jnp.exp(heights), extent[dim] // blocks).reshape((-1,) + (1,) * (len(extent) - 1 - dim))
    return factor_of


def normal_values(own_key, extent, scale, limit, cuts=(), held_as=jnp.bfloat16):
    values = scale * jax.random.normal(own_key, extent, jnp.float32)
    if cuts:
        values = values * level_of(own_key, extent, cuts, -0.22, 0.18)
    return jnp.clip(values, -limit, limit).astype(held_as)


def setup_inputs(seed: int = 0) -> dict:
    arg_keys = jax.random.split(jax.random.key(seed), 7)
    queries = draw_queries(jax.random.fold_in(arg_keys[6], 71), 0)
    keys = draw_keys(jax.random.fold_in(arg_keys[6], 71), 0)
    values = normal_values(arg_keys[2], (TOKENS, HEADS * DH), 1.0, 6.0, ((0, 64), (1, 8)))
    image_slots = normal_values(arg_keys[3], (N_FRAME, 2, REF, HEADS * DH), 1.0, 6.0, ((0, 64), (3, 8)))
    owner = jax.random.randint(arg_keys[4], (1,), 0, N_FRAME).astype(jnp.int32)
    pattern = draw_pattern(jax.random.fold_in(arg_keys[6], 71), 0)
    return dict(queries=queries, keys=keys, values=values, image_slots=image_slots, owner=owner, pattern=pattern)


def tile_attend(query, tile_keys, tile_values, valid):
    heads = query.shape[1] // DH
    qh = query.astype(jnp.float32).reshape(query.shape[0], heads, DH)
    kh = tile_keys.astype(jnp.float32).reshape(tile_keys.shape[0], heads, DH)
    vh = tile_values.astype(jnp.float32).reshape(tile_values.shape[0], heads, DH)
    scores = jnp.einsum("qhd,khd->hqk", qh, kh) * (1.0 / (DH ** 0.5))
    masked = jnp.where(valid[None, None, :], scores, -jnp.inf)
    top = jnp.max(masked, axis=2, keepdims=True)
    weights = jnp.where(valid[None, None, :], jnp.exp(scores - top), 0.0)
    total = jnp.sum(weights, axis=2)
    rounded = weights.astype(jnp.bfloat16).astype(jnp.float32)
    summed = jnp.einsum("hqk,khd->qhd", rounded, vh)
    result = summed / jnp.transpose(total)[:, :, None]
    return result.reshape(query.shape[0], heads * DH).astype(jnp.bfloat16)


def reference(queries, keys, values, image_slots, owner, pattern):
    width = queries.shape[1]
    key_tiles = keys.reshape(TILES, TILE, width)
    value_tiles = values.reshape(TILES, TILE, width)
    query_tiles = queries.reshape(TILES, TILE, width)
    image = lax.dynamic_index_in_dim(image_slots, owner[0].astype(jnp.int32), 0, keepdims=False)

    def one_tile(item):
        query, row = item
        index = jnp.clip(row, 0, TILES - 1).astype(jnp.int32)
        tile_keys = jnp.take(key_tiles, index, axis=0).reshape(NB * TILE, width)
        tile_values = jnp.take(value_tiles, index, axis=0).reshape(NB * TILE, width)
        tile_keys = jnp.concatenate([tile_keys, image[0]], axis=0)
        tile_values = jnp.concatenate([tile_values, image[1]], axis=0)
        valid = jnp.concatenate([jnp.repeat(row >= 0, TILE), jnp.ones((REF,), bool)])
        return tile_attend(query, tile_keys, tile_values, valid)

    out = lax.map(one_tile, (query_tiles, pattern))
    return out.reshape(TOKENS, width)
```

```python
import jax
import jax.numpy as jnp
from jax import lax
from jax.experimental import pallas as pl
from jax.experimental.pallas import tpu as pltpu
from jax.sharding import PartitionSpec as P

DH = 128
TILE = 256
SCALE = 1.4426950408889634 / DH**0.5
NEG = -1e30
F32 = jnp.float32
BF16 = jnp.bfloat16
NX, NY = 4, 8


def at(x, y, z):
    return (x % NX) * (2 * NY) + (y % NY) * 2 + z


FRAMES = [(x, y, z) for x in range(NX) for y in range(NY) for z in range(2)]
FLIP = [(at(x, y, z), at(x, y, 1 - z)) for x, y, z in FRAMES]
ONWARD = [(f, f + 2) for f in range(0, 62, 2)] + [(f, f - 2) for f in range(3, 64, 2)]
DIAGONAL = [(at(x, y, z), at(x, y + 1 - 2 * z, 1 - z)) for x, y, z in FRAMES]
Y_GROUPS = [[at(x, y, z) for y in range(NY)] for x in range(NX) for z in range(2)]


X_GROUPS = [[at(x, y, z) for x in range(NX)] for y in range(NY) for z in range(2)]


def permute(value, pairs):
    return lax.ppermute(value, "frame", pairs)


def exchange(value, groups):
    return lax.all_to_all(value, "frame", 0, 0, axis_index_groups=groups, tiled=True)


def copies(value, count):
    return jnp.broadcast_to(value[None], (count,) + value.shape)


def scores_of(q, k):
    return lax.dot_general(q, k, (((1,), (1,)), ((), ())), preferred_element_type=F32)


def peak_of(r):
    top = r[:, :DH]
    for i in range(DH, r.shape[1], DH):
        top = jnp.maximum(top, r[:, i : i + DH])
    return top


def attend(q, blocks, state):
    raw = [scores_of(q, k) for k, _, _ in blocks]
    peak = None
    for r, (_, _, bias) in zip(raw, blocks):
        here = peak_of(r) * SCALE + bias
        peak = here if peak is None else jnp.maximum(peak, here)
    top = jnp.max(peak, axis=1, keepdims=True)
    if state is not None:
        top = jnp.maximum(state[0], top)
    both = None
    for r, (_, v, bias) in zip(raw, blocks):
        p = jnp.exp2(r * SCALE - (top - bias)).astype(BF16)
        wide = jnp.concatenate([v, jnp.ones_like(v)], axis=1)
        part = jnp.dot(p, wide, preferred_element_type=F32)
        both = part if both is None else both + part
    total, summed = both[:, DH : DH + 1], both[:, :DH]
    if state is not None:
        fade = jnp.exp2(state[0] - top)
        total, summed = state[1] * fade + total, state[2] * fade + summed
    return top, total, summed


def lanes(rows):
    return lax.broadcasted_iota(jnp.int32, (rows, DH), 1)


def put_stats(ref, rows, h, top, total):
    lane = lanes(TILE)
    old = jnp.where(h == 0, 0.0, ref[rows, :])
    ref[rows, :] = jnp.where(lane == h, top, jnp.where(lane == h + DH // 2, total, old))


def get_stats(ref, rows, h):
    lane, held = lanes(TILE), ref[rows, :]
    top = jnp.sum(jnp.where(lane == h, held, 0.0), axis=1, keepdims=True)
    total = jnp.sum(jnp.where(lane == h + DH // 2, held, 0.0), axis=1, keepdims=True)
    return top, total


def finished(total, summed):
    return (summed * (1.0 / total)).astype(BF16)


def tile_rows(tile):
    return pl.ds(pl.multiple_of(tile * TILE, TILE), TILE)


def pack_kernel(_, *refs):
    count = len(refs) // 3
    for i in range(count):
        refs[2 * count + i][0] = refs[2 * i][...]
        refs[2 * count + i][1] = refs[2 * i + 1][...]


def fan_kernel(one, out):
    out[0] = one[...]


def own_kernel(bias, q, k, v, summed_ref, stats_ref):
    h = pl.program_id(0)
    for t in range(3):
        rows = pl.ds(t * TILE, TILE)
        blocks = [
            (k[pl.ds(u * TILE, TILE), :], v[pl.ds(u * TILE, TILE), :], bias[t, u - t + 2])
            for u in range(3)
        ]
        top, total, summed = attend(q[rows, :], blocks, None)
        summed_ref[rows, :] = summed
        put_stats(stats_ref, rows, h, top, total)


def last_kernel(side, bias, q, summed, stats, image, far, mid, fwd, near, out):
    h, p = pl.program_id(0), side[0]
    image_k = image[:, :, 0].reshape(4 * DH, DH)
    image_v = image[:, :, 1].reshape(4 * DH, DH)
    extra = (
        ((far, 1), (fwd, 0)),
        ((far, 0), (near, 4)),
        ((near, 3), (mid, 4)),
    )
    for r in range(3):
        rows = tile_rows(jnp.where(p == 0, r, 2 - r))
        blocks = [(image_k, image_v, 0.0)]
        blocks += [(pair[0], pair[1], bias[r, j]) for pair, j in extra[r]]
        state = get_stats(stats, rows, h) + (summed[rows, :],)
        _, total, acc = attend(q[rows, :], blocks, state)
        out[rows, :] = finished(total, acc)


def cost(blocks, heads):
    return pl.CostEstimate(flops=blocks * heads, transcendentals=0, bytes_accessed=blocks)


def tied(*values):
    return lax.optimization_barrier(values)


def per_device(queries, keys, values, image_slots, owner, pattern):
    rows, width = queries.shape
    heads = width // DH
    frame = lax.axis_index("frame")
    side = frame & 1
    owner_x, owner_y, owner_z = owner[0] // (2 * NY), (owner[0] // 2) % NY, owner[0] % 2
    sides = side.astype(jnp.int32).reshape(1)
    shown = jnp.where(pattern >= 0, 0.0, NEG).astype(F32)
    mirrored = jnp.where(side == 0, shown, shown[::-1, ::-1])
    smem = pl.BlockSpec(memory_space=pltpu.SMEM)
    anywhere = pl.BlockSpec(memory_space=pl.ANY)
    roomy = pltpu.CompilerParams(vmem_limit_bytes=60 * 2**20)

    def pack(*tiles):
        places = jnp.stack([jnp.broadcast_to(t, ()).astype(jnp.int32) for t in tiles])
        ins = [
            pl.BlockSpec((TILE, width), lambda i, t, n=n: (t[n], 0))
            for n in range(len(tiles))
            for _ in range(2)
        ]
        outs = pl.BlockSpec((2, TILE, width), lambda i, t: (0, 0, 0))
        return pl.pallas_call(
            pack_kernel,
            grid_spec=pltpu.PrefetchScalarGridSpec(
                num_scalar_prefetch=1, grid=(1,), in_specs=ins, out_specs=[outs] * len(tiles)
            ),
            out_shape=[jax.ShapeDtypeStruct((2, TILE, width), BF16)] * len(tiles),
            cost_estimate=cost(1, 1),
            compiler_params=roomy,
            name="pack_tiles",
        )(places, *([keys, values] * len(tiles)))

    def whole(h, *_):
        return (0, h)

    def fixed(h, *_):
        return (0, 0)

    pair = pl.BlockSpec((2, TILE, DH), lambda h, s: (0, 0, h))
    every = pl.BlockSpec((rows, DH), whole)
    every_stats = pl.BlockSpec((rows, DH), fixed)
    state_shape = [
        jax.ShapeDtypeStruct((rows, width), F32),
        jax.ShapeDtypeStruct((rows, DH), F32),
    ]

    far, mid = pack(2 * side, 1)
    far, mid = permute(far, FLIP), permute(mid, FLIP)

    slot = image_slots[0].reshape(2, NX, NY, 512 // (NX * NY), width)
    quarters = exchange(jnp.transpose(slot, (1, 2, 0, 3, 4)), X_GROUPS)
    quarter = lax.dynamic_index_in_dim(quarters, owner_x, 0, keepdims=False)

    def scattered(quarter, q, k, v):
        pieces = exchange(quarter, Y_GROUPS)
        summed, stats = pl.pallas_call(
            own_kernel,
            grid=(heads,),
            in_specs=[smem, every, every, every],
            out_specs=[every, every_stats],
            out_shape=state_shape,
            cost_estimate=cost(9, heads),
            compiler_params=roomy,
            name="own_tiles",
        )(shown, q, k, v)
        pieces, summed, stats = tied(pieces, summed, stats)
        piece = lax.dynamic_index_in_dim(pieces, owner_y, 0, keepdims=False)
        piece = jnp.where(side == owner_z, piece, permute(piece, DIAGONAL))
        return piece, summed, stats

    def nothing(function):
        def run(*operands):
            shapes = jax.eval_shape(function, *operands)
            return jax.tree.map(lambda a: jnp.zeros(a.shape, a.dtype), shapes)

        return run

    always = owner[0] >= 0
    piece, summed, stats = lax.cond(
        always, scattered, nothing(scattered), quarter, queries, keys, values
    )
    column = exchange(copies(piece, NY), Y_GROUPS)
    far = permute(tied(far, piece)[0], ONWARD)
    fwd = permute(tied(mid, piece)[0], ONWARD)
    near = permute(pack(2 - 2 * side)[0], FLIP)

    fan = pl.pallas_call(
        fan_kernel,
        grid=(NX,),
        in_specs=[pl.BlockSpec(column.shape, lambda i: (0, 0, 0, 0))],
        out_specs=pl.BlockSpec((1,) + column.shape, lambda i: (i, 0, 0, 0, 0)),
        out_shape=jax.ShapeDtypeStruct((NX,) + column.shape, BF16),
        cost_estimate=pl.CostEstimate(flops=6 * 10**9, transcendentals=0, bytes_accessed=0),
        compiler_params=roomy,
        name="fan_out",
    )(column)

    def gathered(fan):
        return exchange(fan, X_GROUPS)

    image = lax.cond(always, gathered, nothing(gathered), fan)

    return pl.pallas_call(
        last_kernel,
        grid_spec=pltpu.PrefetchScalarGridSpec(
            num_scalar_prefetch=1,
            grid=(heads,),
            in_specs=[smem, every, every, every_stats]
            + [pl.BlockSpec((NX, NY, 2, 16, DH), lambda h, s: (0, 0, 0, 0, h))]
            + [pair] * 4,
            out_specs=every,
        ),
        out_shape=jax.ShapeDtypeStruct((rows, width), BF16),
        cost_estimate=cost(12, heads),
        compiler_params=roomy,
        name="image_and_halo",
    )(sides, mirrored, queries, summed, stats, image, far, mid, fwd, near)


def solution(mesh):
    in_specs = (
        P("frame", "head"),
        P("frame", "head"),
        P("frame", "head"),
        P("frame", None, None, "head"),
        P(),
        P("frame", None),
    )
    out_specs = P("frame", "head")
    return jax.shard_map(
        per_device, mesh=mesh, in_specs=in_specs, out_specs=out_specs, check_vma=False
    )
```

```python
import jax
import jax.numpy as jnp
from jax import lax
from jax.experimental import pallas as pl
from jax.experimental.pallas import tpu as pltpu
from jax.sharding import PartitionSpec as P

DH = 128
TILE = 256
SCALE = 1.4426950408889634 / DH**0.5
NEG = -1e30
F32 = jnp.float32
BF16 = jnp.bfloat16
NX, NY = 4, 8


def at(x, y, z):
    return (x % NX) * (2 * NY) + (y % NY) * 2 + z


FRAMES = [(x, y, z) for x in range(NX) for y in range(NY) for z in range(2)]
FLIP = [(at(x, y, z), at(x, y, 1 - z)) for x, y, z in FRAMES]
ONWARD = [(f, f + 2) for f in range(0, 62, 2)] + [(f, f - 2) for f in range(3, 64, 2)]
BEFORE = [(f, f + 2) for f in range(1, 62, 2)] + [(f, f - 2) for f in range(2, 64, 2)]
DIAGONAL = [(at(x, y, z), at(x, y + 1 - 2 * z, 1 - z)) for x, y, z in FRAMES]
Y_GROUPS = [[at(x, y, z) for y in range(NY)] for x in range(NX) for z in range(2)]


X_GROUPS = [[at(x, y, z) for x in range(NX)] for y in range(NY) for z in range(2)]


def permute(value, pairs):
    return lax.ppermute(value, "frame", pairs)


def exchange(value, groups):
    return lax.all_to_all(value, "frame", 0, 0, axis_index_groups=groups, tiled=True)


def copies(value, count):
    return jnp.broadcast_to(value[None], (count,) + value.shape)


def scores_of(q, k):
    return lax.dot_general(q, k, (((1,), (1,)), ((), ())), preferred_element_type=F32)


def peak_of(r):
    top = r[:, :DH]
    for i in range(DH, r.shape[1], DH):
        top = jnp.maximum(top, r[:, i : i + DH])
    return top


def attend(q, blocks, state):
    raw = [scores_of(q, k) for k, _, _ in blocks]
    peak = None
    for r, (_, _, bias) in zip(raw, blocks):
        here = peak_of(r) * SCALE + bias
        peak = here if peak is None else jnp.maximum(peak, here)
    top = jnp.max(peak, axis=1, keepdims=True)
    if state is not None:
        top = jnp.maximum(state[0], top)
    both = None
    for r, (_, v, bias) in zip(raw, blocks):
        p = jnp.exp2(r * SCALE - (top - bias)).astype(BF16)
        wide = jnp.concatenate([v, jnp.ones_like(v)], axis=1)
        part = jnp.dot(p, wide, preferred_element_type=F32)
        both = part if both is None else both + part
    total, summed = both[:, DH : DH + 1], both[:, :DH]
    if state is not None:
        fade = jnp.exp2(state[0] - top)
        total, summed = state[1] * fade + total, state[2] * fade + summed
    return top, total, summed


def lanes(rows):
    return lax.broadcasted_iota(jnp.int32, (rows, DH), 1)


def put_stats(ref, rows, h, top, total):
    lane = lanes(TILE)
    old = jnp.where(h == 0, 0.0, ref[rows, :])
    ref[rows, :] = jnp.where(lane == h, top, jnp.where(lane == h + DH // 2, total, old))


def get_stats(ref, rows, h):
    lane, held = lanes(TILE), ref[rows, :]
    top = jnp.sum(jnp.where(lane == h, held, 0.0), axis=1, keepdims=True)
    total = jnp.sum(jnp.where(lane == h + DH // 2, held, 0.0), axis=1, keepdims=True)
    return top, total


def finished(total, summed):
    return (summed * (1.0 / total)).astype(BF16)


def tile_rows(tile):
    return pl.ds(pl.multiple_of(tile * TILE, TILE), TILE)


def pack_kernel(_, *refs):
    count = len(refs) // 3
    for i in range(count):
        refs[2 * count + i][0] = refs[2 * i][...]
        refs[2 * count + i][1] = refs[2 * i + 1][...]


def own_kernel(bias, q, k, v, summed_ref, stats_ref):
    h = pl.program_id(0)
    for t in range(3):
        rows = pl.ds(t * TILE, TILE)
        blocks = [
            (k[pl.ds(u * TILE, TILE), :], v[pl.ds(u * TILE, TILE), :], bias[t, u - t + 2])
            for u in range(3)
        ]
        top, total, summed = attend(q[rows, :], blocks, None)
        summed_ref[rows, :] = summed
        put_stats(stats_ref, rows, h, top, total)


def hold_kernel(stats, arrived, out):
    pass


def last_kernel(side, bias, q, summed, stats, image, far, mid, fwd, near, out):
    h, p = pl.program_id(0), side[0]
    image_k = image[:, :, 0].reshape(4 * DH, DH)
    image_v = image[:, :, 1].reshape(4 * DH, DH)
    extra = (
        ((far, 1), (fwd, 0)),
        ((far, 0), (near, 4)),
        ((near, 3), (mid, 4)),
    )
    for r in range(3):
        rows = tile_rows(jnp.where(p == 0, r, 2 - r))
        blocks = [(image_k, image_v, 0.0)]
        blocks += [(pair[0], pair[1], bias[r, j]) for pair, j in extra[r]]
        state = get_stats(stats, rows, h) + (summed[rows, :],)
        _, total, acc = attend(q[rows, :], blocks, state)
        out[rows, :] = finished(total, acc)


def cost(blocks, heads):
    return pl.CostEstimate(flops=blocks * heads, transcendentals=0, bytes_accessed=blocks)


def tied(*values):
    return lax.optimization_barrier(values)


def per_device(queries, keys, values, image_slots, owner, pattern):
    rows, width = queries.shape
    heads = width // DH
    frame = lax.axis_index("frame")
    side = frame & 1
    owner_x, owner_y, owner_z = owner[0] // (2 * NY), (owner[0] // 2) % NY, owner[0] % 2
    sides = side.astype(jnp.int32).reshape(1)
    shown = jnp.where(pattern >= 0, 0.0, NEG).astype(F32)
    mirrored = jnp.where(side == 0, shown, shown[::-1, ::-1])
    smem = pl.BlockSpec(memory_space=pltpu.SMEM)
    anywhere = pl.BlockSpec(memory_space=pl.ANY)
    roomy = pltpu.CompilerParams(vmem_limit_bytes=60 * 2**20)

    def pack(*tiles):
        places = jnp.stack([jnp.broadcast_to(t, ()).astype(jnp.int32) for t in tiles])
        ins = [
            pl.BlockSpec((TILE, width), lambda i, t, n=n: (t[n], 0))
            for n in range(len(tiles))
            for _ in range(2)
        ]
        outs = pl.BlockSpec((2, TILE, width), lambda i, t: (0, 0, 0))
        return pl.pallas_call(
            pack_kernel,
            grid_spec=pltpu.PrefetchScalarGridSpec(
                num_scalar_prefetch=1, grid=(1,), in_specs=ins, out_specs=[outs] * len(tiles)
            ),
            out_shape=[jax.ShapeDtypeStruct((2, TILE, width), BF16)] * len(tiles),
            cost_estimate=cost(1, 1),
            compiler_params=roomy,
            name="pack_tiles",
        )(places, *([keys, values] * len(tiles)))

    def whole(h, *_):
        return (0, h)

    def fixed(h, *_):
        return (0, 0)

    pair = pl.BlockSpec((2, TILE, DH), lambda h, s: (0, 0, h))
    every = pl.BlockSpec((rows, DH), whole)
    every_stats = pl.BlockSpec((rows, DH), fixed)
    state_shape = [
        jax.ShapeDtypeStruct((rows, width), F32),
        jax.ShapeDtypeStruct((rows, DH), F32),
    ]

    far, mid, near = pack(2 * side, 1, 2 - 2 * side)
    mid, near = permute(mid, FLIP), permute(near, FLIP)

    slot = image_slots[0].reshape(2, NX, NY, 512 // (NX * NY), width)
    quarters = exchange(jnp.transpose(slot, (1, 2, 0, 3, 4)), X_GROUPS)
    quarter = lax.dynamic_index_in_dim(quarters, owner_x, 0, keepdims=False)

    def scattered(quarter, far, q, k, v):
        far = permute(far, BEFORE)
        pieces = exchange(quarter, Y_GROUPS)
        summed, stats = pl.pallas_call(
            own_kernel,
            grid=(heads,),
            in_specs=[smem, every, every, every],
            out_specs=[every, every_stats],
            out_shape=state_shape,
            cost_estimate=cost(9, heads),
            compiler_params=roomy,
            name="own_tiles",
        )(shown, q, k, v)
        pieces, summed, stats = tied(pieces, summed, stats)
        piece = lax.dynamic_index_in_dim(pieces, owner_y, 0, keepdims=False)
        piece = jnp.where(side == owner_z, piece, permute(piece, DIAGONAL))
        return piece, far, summed, stats

    def nothing(function):
        def run(*operands):
            shapes = jax.eval_shape(function, *operands)
            return jax.tree.map(lambda a: jnp.zeros(a.shape, a.dtype), shapes)

        return run

    always = owner[0] >= 0
    piece, far, summed, stats = lax.cond(
        always, scattered, nothing(scattered), quarter, far, queries, keys, values
    )
    far = permute(far, FLIP)

    mid, piece = tied(mid, piece)
    fwd = permute(mid, ONWARD)

    def gathered(piece):
        column = exchange(copies(piece, NY), Y_GROUPS)
        return exchange(copies(column, NX), X_GROUPS)

    image = lax.cond(always, gathered, nothing(gathered), piece)

    def held(stats, arrived):
        return pl.pallas_call(
            hold_kernel,
            in_specs=[pl.BlockSpec(memory_space=pltpu.HBM)] * 2,
            out_specs=pl.BlockSpec(memory_space=pltpu.HBM),
            out_shape=state_shape[1],
            input_output_aliases={0: 0},
            compiler_params=pltpu.CompilerParams(vmem_limit_bytes=63 * 2**20),
            cost_estimate=pl.CostEstimate(flops=3 * 10**9, transcendentals=0, bytes_accessed=0),
            name="hold",
        )(stats, arrived)

    far, stats = tied(far, held(stats, near))
    fwd, stats = tied(fwd, held(stats, far))

    return pl.pallas_call(
        last_kernel,
        grid_spec=pltpu.PrefetchScalarGridSpec(
            num_scalar_prefetch=1,
            grid=(heads,),
            in_specs=[smem, every, every, every_stats]
            + [pl.BlockSpec((NX, NY, 2, 16, DH), lambda h, s: (0, 0, 0, 0, h))]
            + [pair] * 4,
            out_specs=every,
        ),
        out_shape=jax.ShapeDtypeStruct((rows, width), BF16),
        cost_estimate=cost(12, heads),
        compiler_params=pltpu.CompilerParams(vmem_limit_bytes=63 * 2**20),
        name="image_and_halo",
    )(sides, mirrored, queries, summed, stats, image, far, mid, fwd, near)


def solution(mesh):
    in_specs = (
        P("frame", "head"),
        P("frame", "head"),
        P("frame", "head"),
        P("frame", None, None, "head"),
        P(),
        P("frame", None),
    )
    out_specs = P("frame", "head")
    return jax.shard_map(
        per_device, mesh=mesh, in_specs=in_specs, out_specs=out_specs, check_vma=False
    )
```

```python
import jax
import jax.numpy as jnp
from jax import lax
from jax.experimental import pallas as pl
from jax.experimental.pallas import tpu as pltpu
from jax.sharding import PartitionSpec as P

DH = 128
TILE = 256
SCALE = 1.4426950408889634 / DH**0.5
NEG = -1e30
F32 = jnp.float32
BF16 = jnp.bfloat16
NX, NY = 4, 8


def at(x, y, z):
    return (x % NX) * (2 * NY) + (y % NY) * 2 + z


FRAMES = [(x, y, z) for x in range(NX) for y in range(NY) for z in range(2)]
FLIP = [(at(x, y, z), at(x, y, 1 - z)) for x, y, z in FRAMES]
ONWARD = [(f, f + 2) for f in range(0, 62, 2)] + [(f, f - 2) for f in range(3, 64, 2)]
BEFORE = [(f, f + 2) for f in range(1, 62, 2)] + [(f, f - 2) for f in range(2, 64, 2)]
DIAGONAL = [(at(x, y, z), at(x, y + 1 - 2 * z, 1 - z)) for x, y, z in FRAMES]
Y_GROUPS = [[at(x, y, z) for y in range(NY)] for x in range(NX) for z in range(2)]


X_GROUPS = [[at(x, y, z) for x in range(NX)] for y in range(NY) for z in range(2)]


def permute(value, pairs):
    return lax.ppermute(value, "frame", pairs)


def exchange(value, groups):
    return lax.all_to_all(value, "frame", 0, 0, axis_index_groups=groups, tiled=True)


def copies(value, count):
    return jnp.broadcast_to(value[None], (count,) + value.shape)


def scores_of(q, k):
    return lax.dot_general(q, k, (((1,), (1,)), ((), ())), preferred_element_type=F32)


def peak_of(r):
    top = r[:, :DH]
    for i in range(DH, r.shape[1], DH):
        top = jnp.maximum(top, r[:, i : i + DH])
    return top


def attend(q, blocks, state):
    raw = [scores_of(q, k) for k, _, _ in blocks]
    peak = None
    for r, (_, _, bias) in zip(raw, blocks):
        here = peak_of(r) * SCALE + bias
        peak = here if peak is None else jnp.maximum(peak, here)
    top = jnp.max(peak, axis=1, keepdims=True)
    if state is not None:
        top = jnp.maximum(state[0], top)
    both = None
    for r, (_, v, bias) in zip(raw, blocks):
        p = jnp.exp2(r * SCALE - (top - bias)).astype(BF16)
        wide = jnp.concatenate([v, jnp.ones_like(v)], axis=1)
        part = jnp.dot(p, wide, preferred_element_type=F32)
        both = part if both is None else both + part
    total, summed = both[:, DH : DH + 1], both[:, :DH]
    if state is not None:
        fade = jnp.exp2(state[0] - top)
        total, summed = state[1] * fade + total, state[2] * fade + summed
    return top, total, summed


def lanes(rows):
    return lax.broadcasted_iota(jnp.int32, (rows, DH), 1)


def put_stats(ref, rows, h, top, total):
    lane = lanes(TILE)
    old = jnp.where(h == 0, 0.0, ref[rows, :])
    ref[rows, :] = jnp.where(lane == h, top, jnp.where(lane == h + DH // 2, total, old))


def get_stats(ref, rows, h):
    lane, held = lanes(TILE), ref[rows, :]
    top = jnp.sum(jnp.where(lane == h, held, 0.0), axis=1, keepdims=True)
    total = jnp.sum(jnp.where(lane == h + DH // 2, held, 0.0), axis=1, keepdims=True)
    return top, total


def finished(total, summed):
    return (summed * (1.0 / total)).astype(BF16)


def tile_rows(tile):
    return pl.ds(pl.multiple_of(tile * TILE, TILE), TILE)


def pack_kernel(_, *refs):
    count = len(refs) // 3
    for i in range(count):
        refs[2 * count + i][0] = refs[2 * i][...]
        refs[2 * count + i][1] = refs[2 * i + 1][...]


def fan_kernel(one, out, sems):
    copies = [
        pltpu.make_async_copy(one, out.at[i], sems.at[i]) for i in range(out.shape[0])
    ]
    for c in copies:
        c.start()
    for c in copies:
        c.wait()


def own_kernel(bias, q, k, v, summed_ref, stats_ref):
    h = pl.program_id(0)
    for t in range(3):
        rows = pl.ds(t * TILE, TILE)
        blocks = [
            (k[pl.ds(u * TILE, TILE), :], v[pl.ds(u * TILE, TILE), :], bias[t, u - t + 2])
            for u in range(3)
        ]
        top, total, summed = attend(q[rows, :], blocks, None)
        summed_ref[rows, :] = summed
        put_stats(stats_ref, rows, h, top, total)


def hold_kernel(stats, arrived, out):
    pass


def last_kernel(side, bias, q, summed, stats, image, far, mid, fwd, near, out):
    h, p = pl.program_id(0), side[0]
    image_k = image[:, :, 0].reshape(4 * DH, DH)
    image_v = image[:, :, 1].reshape(4 * DH, DH)
    extra = (
        ((far, 1), (fwd, 0)),
        ((far, 0), (near, 4)),
        ((near, 3), (mid, 4)),
    )
    for r in range(3):
        rows = tile_rows(jnp.where(p == 0, r, 2 - r))
        blocks = [(image_k, image_v, 0.0)]
        blocks += [(pair[0], pair[1], bias[r, j]) for pair, j in extra[r]]
        state = get_stats(stats, rows, h) + (summed[rows, :],)
        _, total, acc = attend(q[rows, :], blocks, state)
        out[rows, :] = finished(total, acc)


def cost(blocks, heads):
    return pl.CostEstimate(flops=blocks * heads, transcendentals=0, bytes_accessed=blocks)


def tied(*values):
    return lax.optimization_barrier(values)


def per_device(queries, keys, values, image_slots, owner, pattern):
    rows, width = queries.shape
    heads = width // DH
    frame = lax.axis_index("frame")
    side = frame & 1
    owner_x, owner_y, owner_z = owner[0] // (2 * NY), (owner[0] // 2) % NY, owner[0] % 2
    sides = side.astype(jnp.int32).reshape(1)
    shown = jnp.where(pattern >= 0, 0.0, NEG).astype(F32)
    mirrored = jnp.where(side == 0, shown, shown[::-1, ::-1])
    smem = pl.BlockSpec(memory_space=pltpu.SMEM)
    anywhere = pl.BlockSpec(memory_space=pl.ANY)
    roomy = pltpu.CompilerParams(vmem_limit_bytes=60 * 2**20)

    def pack(*tiles):
        places = jnp.stack([jnp.broadcast_to(t, ()).astype(jnp.int32) for t in tiles])
        ins = [
            pl.BlockSpec((TILE, width), lambda i, t, n=n: (t[n], 0))
            for n in range(len(tiles))
            for _ in range(2)
        ]
        outs = pl.BlockSpec((2, TILE, width), lambda i, t: (0, 0, 0))
        return pl.pallas_call(
            pack_kernel,
            grid_spec=pltpu.PrefetchScalarGridSpec(
                num_scalar_prefetch=1, grid=(1,), in_specs=ins, out_specs=[outs] * len(tiles)
            ),
            out_shape=[jax.ShapeDtypeStruct((2, TILE, width), BF16)] * len(tiles),
            cost_estimate=cost(1, 1),
            compiler_params=roomy,
            name="pack_tiles",
        )(places, *([keys, values] * len(tiles)))

    def whole(h, *_):
        return (0, h)

    def fixed(h, *_):
        return (0, 0)

    pair = pl.BlockSpec((2, TILE, DH), lambda h, s: (0, 0, h))
    every = pl.BlockSpec((rows, DH), whole)
    every_stats = pl.BlockSpec((rows, DH), fixed)
    state_shape = [
        jax.ShapeDtypeStruct((rows, width), F32),
        jax.ShapeDtypeStruct((rows, DH), F32),
    ]

    far, mid, near = pack(2 * side, 1, 2 - 2 * side)
    mid, near = permute(mid, FLIP), permute(near, FLIP)

    slot = image_slots[0].reshape(2, NX, NY, 512 // (NX * NY), width)
    quarters = exchange(jnp.transpose(slot, (1, 2, 0, 3, 4)), X_GROUPS)
    quarter = lax.dynamic_index_in_dim(quarters, owner_x, 0, keepdims=False)

    def scattered(quarter, far, q, k, v):
        far = permute(far, BEFORE)
        pieces = exchange(quarter, Y_GROUPS)
        summed, stats = pl.pallas_call(
            own_kernel,
            grid=(heads,),
            in_specs=[smem, every, every, every],
            out_specs=[every, every_stats],
            out_shape=state_shape,
            cost_estimate=cost(9, heads),
            compiler_params=roomy,
            name="own_tiles",
        )(shown, q, k, v)
        pieces, summed, stats = tied(pieces, summed, stats)
        piece = lax.dynamic_index_in_dim(pieces, owner_y, 0, keepdims=False)
        piece = jnp.where(side == owner_z, piece, permute(piece, DIAGONAL))
        return piece, far, summed, stats

    def nothing(function):
        def run(*operands):
            shapes = jax.eval_shape(function, *operands)
            return jax.tree.map(lambda a: jnp.zeros(a.shape, a.dtype), shapes)

        return run

    always = owner[0] >= 0
    piece, far, summed, stats = lax.cond(
        always, scattered, nothing(scattered), quarter, far, queries, keys, values
    )
    column = exchange(copies(piece, NY), Y_GROUPS)
    column, near = tied(column, near)
    fwd = permute(tied(mid, piece)[0], ONWARD)
    far = permute(far, FLIP)

    fan = pl.pallas_call(
        fan_kernel,
        in_specs=[pl.BlockSpec(memory_space=pltpu.VMEM)],
        out_specs=pl.BlockSpec(memory_space=pltpu.HBM),
        out_shape=jax.ShapeDtypeStruct((NX,) + column.shape, BF16),
        scratch_shapes=[pltpu.SemaphoreType.DMA((NX,))],
        cost_estimate=pl.CostEstimate(flops=6 * 10**9, transcendentals=0, bytes_accessed=0),
        compiler_params=roomy,
        name="fan_out",
    )(column)

    def gathered(fan):
        return exchange(fan, X_GROUPS)

    image = lax.cond(always, gathered, nothing(gathered), fan)

    def held(stats, arrived):
        return pl.pallas_call(
            hold_kernel,
            in_specs=[pl.BlockSpec(memory_space=pltpu.HBM)] * 2,
            out_specs=pl.BlockSpec(memory_space=pltpu.HBM),
            out_shape=state_shape[1],
            input_output_aliases={0: 0},
            compiler_params=pltpu.CompilerParams(vmem_limit_bytes=63 * 2**20),
            cost_estimate=pl.CostEstimate(flops=3 * 10**9, transcendentals=0, bytes_accessed=0),
            name="hold",
        )(stats, arrived)

    fwd, stats = tied(fwd, held(stats, far))

    return pl.pallas_call(
        last_kernel,
        grid_spec=pltpu.PrefetchScalarGridSpec(
            num_scalar_prefetch=1,
            grid=(heads,),
            in_specs=[smem, every, every, every_stats]
            + [pl.BlockSpec((NX, NY, 2, 16, DH), lambda h, s: (0, 0, 0, 0, h))]
            + [pair] * 4,
            out_specs=every,
        ),
        out_shape=jax.ShapeDtypeStruct((rows, width), BF16),
        cost_estimate=cost(12, heads),
        compiler_params=pltpu.CompilerParams(vmem_limit_bytes=63 * 2**20),
        name="image_and_halo",
    )(sides, mirrored, queries, summed, stats, image, far, mid, fwd, near)


def solution(mesh):
    in_specs = (
        P("frame", "head"),
        P("frame", "head"),
        P("frame", "head"),
        P("frame", None, None, "head"),
        P(),
        P("frame", None),
    )
    out_specs = P("frame", "head")
    return jax.shard_map(
        per_device, mesh=mesh, in_specs=in_specs, out_specs=out_specs, check_vma=False
    )
```
